32 devices in a mesh: section: 2 (over core), dp: 16 (over z, y, x).
Axes of the slice: x: 2, y: 2, z: 4, core: 2. Of those that a mesh axis runs over, the one named last changes fastest.
Arguments:
- images: bfloat16 [4, 16, 196, 512], P(None, 'dp'), may hold values from -6 to 6
- counts: int32 [4, 16], P(None, 'dp'), may hold values from 1 to 1, as said below
- shift_mask: int32 [4, 49, 49], replicated, may hold values from 0 to 1, as said below
- cotangent: bfloat16 [4, 16, 196, 512], P(None, 'dp'), may hold values from -6 to 6
- attention_gain: bfloat16 [2, 512], P('section', 'dp'), may hold values from 0.5 to 1.5
- attention_shift: bfloat16 [2, 512], P('section', 'dp'), may hold values from -3 to 3
- heads_weight: bfloat16 [2, 512, 1536], P('section', 'dp'), may hold values from -0.25 to 0.25
- query_bias: bfloat16 [2, 512], P('section', 'dp'), may hold values from -3 to 3
- value_bias: bfloat16 [2, 512], P('section', 'dp'), may hold values from -3 to 3
- merge_weight: bfloat16 [2, 512, 512], P('section', 'dp'), may hold values from -1 to 1
- merge_bias: bfloat16 [2, 512], P('section', 'dp'), may hold values from -3 to 3
- feed_gain: bfloat16 [2, 512], P('section', 'dp'), may hold values from 0.5 to 1.5
- feed_shift: bfloat16 [2, 512], P('section', 'dp'), may hold values from -3 to 3
- up_weight: bfloat16 [2, 512, 2048], P('section', 'dp'), may hold values from -0.25 to 0.25
- up_bias: bfloat16 [2, 2048], P('section', 'dp'), may hold values from -3 to 3
- down_weight: bfloat16 [2, 2048, 512], P('section', 'dp'), may hold values from -0.125 to 0.125
- down_bias: bfloat16 [2, 512], P('section', 'dp'), may hold values from -3 to 3
- bias_table: bfloat16 [2, 169, 16], P('section'), may hold values from -5 to 5
Outputs:
- layer_outputs: bfloat16 [2, 4, 16, 196, 512], P('section', None, 'dp')
- input_grads: float32 [2, 4, 16, 196, 512], P('section', None, 'dp')
- grad_attention_gain: float32 [2, 512], P('section', 'dp')
- grad_attention_shift: float32 [2, 512], P('section', 'dp')
- grad_heads_weight: float32 [2, 512, 1536], P('section', 'dp')
- grad_query_bias: float32 [2, 512], P('section', 'dp')
- grad_value_bias: float32 [2, 512], P('section', 'dp')
- grad_merge_weight: float32 [2, 512, 512], P('section', 'dp')
- grad_merge_bias: float32 [2, 512], P('section', 'dp')
- grad_feed_gain: float32 [2, 512], P('section', 'dp')
- grad_feed_shift: float32 [2, 512], P('section', 'dp')
- grad_up_weight: float32 [2, 512, 2048], P('section', 'dp')
- grad_up_bias: float32 [2, 2048], P('section', 'dp')
- grad_down_weight: float32 [2, 2048, 512], P('section', 'dp')
- grad_down_bias: float32 [2, 512], P('section', 'dp')
- grad_bias_table: float32 [2, 169, 16], P('section')
The draws below stay inside these ranges and needn't reach their ends.
Inputs may be any that keep to these rules, and one draw needn't show every extreme that they name: Device d has 1 image slots in each micro-batch m, of which the first counts[m, d] hold images and the rest are empty; in every micro-batch some device fills all 1. `shift_mask`: for each window position, one row cut and one column cut split the window's tokens into rectangles; the mask is 1 between tokens of different rectangles and 0 within one (so symmetric, 0 on the diagonal).
All inputs are finite; a program needn't handle non-finite values.
Results may differ from the reference program's by a relative error of at most 0.017.
Values may be sent and summed in bfloat16 or wider, within the bound.
A program may use at most 192 MiB of HBM per device.

```python
import jax
import jax.numpy as jnp
from jax import lax

C = 512
HEADS = 16
HD = 32
FF = 2048
WIN = 7
SIDE = 14
SHIFT = 3
MICRO = 4
IMG_DEV = 1
WT = 49
NWIN = 4
TOKIMG = 196
TABLE = 169
IMAGES = 16


def draw_counts(key, part):
    key = jax.random.fold_in(key, 11)
    key_sample, key_fullest = jax.random.split(key)
    devices = IMAGES // IMG_DEV
    sampled = jax.random.randint(key_sample, (MICRO, devices), 1, IMG_DEV + 1, dtype=jnp.int32)
    fullest = jax.random.randint(key_fullest, (MICRO, 1), 0, devices, dtype=jnp.int32)
    columns = jnp.arange(devices, dtype=jnp.int32)[None, :]
    return jnp.where(columns == fullest, IMG_DEV, sampled).astype(jnp.int32)


def draw_shift_mask(key, part):
    key = jax.random.fold_in(key, 23)
    key_rows, key_cols = jax.random.split(key)
    row_cut = jax.random.randint(key_rows, (NWIN, 1), 1, WIN, dtype=jnp.int32)
    col_cut = jax.random.randint(key_cols, (NWIN, 1), 1, WIN, dtype=jnp.int32)
    position = jnp.arange(WT, dtype=jnp.int32)[None, :]
    labels = 2 * (position // WIN >= row_cut).astype(jnp.int32) + (position % WIN >= col_cut).astype(jnp.int32)
    return (labels[:, :, None] != labels[:, None, :]).astype(jnp.int32)


def shard_levels(key, dims, cuts, least, top_value):
    loudness, own = 1.0, jax.random.fold_in(key, 6)
    for dim, shards_of in cuts:
        draws = jnp.exp(jax.random.uniform(jax.random.fold_in(own, dim), (shards_of,), jnp.float32, least / len(cuts), top_value / len(cuts)))
        loudness = loudness * jnp.repeat(draws, dims[dim] // shards_of).reshape([-1 if axis == dim else 1 for axis in range(len(dims))])
    return loudness


def centred(key, shape, scale, reach, pieces=(), kind=jnp.bfloat16):
    loudness = shard_levels(key, shape, pieces, -0.22, 0.18) if pieces else 1.0
    entries = jax.random.normal(key, shape, jnp.float32) * scale * loudness
    return jnp.minimum(jnp.maximum(entries, -reach), reach).astype(kind)


def setup_inputs(seed: int = 0) -> dict:
    seeds = jax.random.split(jax.random.key(seed), 19)
    return {
        "images": centred(seeds[0], (MICRO, IMAGES, TOKIMG, C), 1.0, 6.0, ((1, 16),)),
        "counts": draw_counts(jax.random.fold_in(seeds[18], 71), 0),
        "shift_mask": draw_shift_mask(jax.random.fold_in(seeds[18], 71), 0),
        "cotangent": centred(seeds[3], (MICRO, IMAGES, TOKIMG, C), 1.0, 6.0, ((1, 16),)),
        "attention_gain": jnp.clip(1.0 + 0.1 * jax.random.normal(seeds[4], (2, C), jnp.float32), 0.5, 1.5).astype(jnp.bfloat16),
        "attention_shift": centred(seeds[5], (2, C), 0.5, 3.0, ((0, 2), (1, 16))),
        "heads_weight": centred(seeds[6], (2, C, 3 * C), C ** -0.5, 0.25, ((0, 2), (1, 16))),
        "query_bias": centred(seeds[7], (2, C), 0.5, 3.0, ((0, 2), (1, 16))),
        "value_bias": centred(seeds[8], (2, C), 0.5, 3.0, ((0, 2), (1, 16))),
        "merge_weight": centred(seeds[9], (2, C, C), (C // 16) ** -0.5, 1.0, ((0, 2), (1, 16))),
        "merge_bias": centred(seeds[10], (2, C), 0.5, 3.0, ((0, 2), (1, 16))),
        "feed_gain": jnp.clip(1.0 + 0.1 * jax.random.normal(seeds[11], (2, C), jnp.float32), 0.5, 1.5).astype(jnp.bfloat16),
        "feed_shift": centred(seeds[12], (2, C), 0.5, 3.0, ((0, 2), (1, 16))),
        "up_weight": centred(seeds[13], (2, C, FF), C ** -0.5, 0.25, ((0, 2), (1, 16))),
        "up_bias": centred(seeds[14], (2, FF), 0.5, 3.0, ((0, 2), (1, 16))),
        "down_weight": centred(seeds[15], (2, FF, C), FF ** -0.5, 0.125, ((0, 2), (1, 16))),
        "down_bias": centred(seeds[16], (2, C), 0.5, 3.0, ((0, 2), (1, 16))),
        "bias_table": centred(seeds[17], (2, TABLE, HEADS), 1.0, 5.0, ((0, 2),)),
    }


@jax.custom_vjp
def low(v):
    return lax.optimization_barrier(v.astype(jnp.bfloat16)).astype(jnp.float32)

@jax.custom_vjp
def low_back(v):
    return v

def low_keep(v):
    return (low(v), None)

def low_pass(kept, grad):
    return (grad,)

def back_keep(v):
    return (v, None)

def back_low(kept, grad):
    return (low(grad),)
low.defvjp(low_keep, low_pass)
low_back.defvjp(back_keep, back_low)
EPSILON = 1e-05

def layer_norm(values, norm_gain, offset):
    center = values - lax.optimization_barrier(jnp.mean(values, -1, keepdims=True))
    spread = lax.optimization_barrier(jnp.mean(center * center, -1, keepdims=True))
    return center * lax.rsqrt(spread + EPSILON) * norm_gain + offset

def gelu_exact(inputs):
    return jax.nn.gelu(inputs, approximate=False)

def relative_index():
    position = jnp.arange(WT, dtype=jnp.int32)
    rows_of = position // WIN
    cols_of = position % WIN
    return ((rows_of[:, None] - rows_of[None, :] + WIN - 1) * (2 * WIN - 1) + cols_of[:, None] - cols_of[None, :] + WIN - 1).astype(jnp.int32)

def to_windows(tokens, is_second):
    batch_size = tokens.shape[0]
    channels = tokens.shape[-1]
    square = tokens.reshape(batch_size, SIDE, SIDE, channels)
    square = jnp.where(is_second, jnp.roll(square, (-SHIFT, -SHIFT), (1, 2)), square)
    square = square.reshape(batch_size, SIDE // WIN, WIN, SIDE // WIN, WIN, channels)
    return square.transpose(0, 1, 3, 2, 4, 5).reshape(batch_size * NWIN, WT, channels)

def from_windows(windows, is_second):
    batch_size = windows.shape[0] // NWIN
    channels = windows.shape[-1]
    square = windows.reshape(batch_size, SIDE // WIN, SIDE // WIN, WIN, WIN, channels)
    square = square.transpose(0, 1, 3, 2, 4, 5).reshape(batch_size, SIDE, SIDE, channels)
    square = jnp.where(is_second, jnp.roll(square, (SHIFT, SHIFT), (1, 2)), square)
    return square.reshape(batch_size, TOKIMG, channels)

def matmul(former, latter):
    return jnp.matmul(former, latter, precision=lax.Precision.HIGHEST)

def layer(inputs, weights, table, mask_add, is_second):
    attention_gain, attention_shift, heads_weight, query_bias, value_bias, merge_weight, merge_bias, feed_gain, feed_shift, up_weight, up_bias, down_weight, down_bias = weights
    batch_size = inputs.shape[0]
    normed = low(layer_norm(inputs, attention_gain, attention_shift))
    windowed = to_windows(normed, is_second)
    window_count = windowed.shape[0]
    project_bias = jnp.concatenate([query_bias, jnp.zeros((C,), jnp.float32), value_bias])
    projected = low_back(low(matmul(windowed, heads_weight) + project_bias))
    projected = projected.reshape(window_count, WT, 3, HEADS, HD)
    queries = projected[:, :, 0]
    key_vectors = projected[:, :, 1]
    value_vectors = projected[:, :, 2]
    scores = jnp.einsum('wihd,wjhd->whij', queries, key_vectors, precision=lax.Precision.HIGHEST) * HD ** (-0.5)
    pos_bias = table[relative_index()].transpose(2, 0, 1)
    scores = scores.reshape(batch_size, NWIN, HEADS, WT, WT) + pos_bias[None, None] + mask_add[None, :, None]
    scores = low_back(scores.reshape(window_count, HEADS, WT, WT))
    attention = low(jax.nn.softmax(scores, -1))
    mixed = jnp.einsum('whij,wjhd->wihd', attention, value_vectors, precision=lax.Precision.HIGHEST)
    mixed = low_back(low(mixed.reshape(window_count, WT, C)))
    branch = low_back(matmul(mixed, merge_weight) + merge_bias)
    middle = inputs + from_windows(branch, is_second)
    normed_two = low(layer_norm(middle, feed_gain, feed_shift))
    hidden = low_back(matmul(normed_two, up_weight) + up_bias)
    activated = low(gelu_exact(hidden))
    return middle + low_back(matmul(activated, down_weight) + down_bias)

def add_pair(former, latter):
    return former + latter

def reference(images, counts, shift_mask, cotangent, attention_gain, attention_shift, heads_weight, query_bias, value_bias, merge_weight, merge_bias, feed_gain, feed_shift, up_weight, up_bias, down_weight, down_bias, bias_table):
    params = (attention_gain, attention_shift, heads_weight, query_bias, value_bias, merge_weight, merge_bias, feed_gain, feed_shift, up_weight, up_bias, down_weight, down_bias)
    first_params = tuple((member[0].astype(jnp.float32) for member in params))
    second_params = tuple((member[1].astype(jnp.float32) for member in params))
    first_table = bias_table[0].astype(jnp.float32)
    second_table = bias_table[1].astype(jnp.float32)
    mask_add = -100.0 * shift_mask.astype(jnp.float32)
    no_mask = jnp.zeros_like(mask_add)
    groups = MICRO * (IMAGES // IMG_DEV)
    live_rows = (jnp.arange(IMG_DEV, dtype=jnp.int32)[None, :] < counts.reshape(groups, 1)).astype(jnp.float32)
    inputs_all = images.astype(jnp.float32).reshape(groups, IMG_DEV, TOKIMG, C)
    cot_all = cotangent.astype(jnp.float32).reshape(groups, IMG_DEV, TOKIMG, C)

    def step(carry, blocks):
        inputs, cot_block, live_block = blocks
        live_three = live_block[:, None, None]

        def first_layer(values, weights, table):
            return layer(values, weights, table, no_mask, False) * live_three

        def second_layer(values, weights, table):
            return layer(values, weights, table, mask_add, True) * live_three
        first_out, first_back = jax.vjp(first_layer, inputs, first_params, first_table)
        middle_in = low(first_out)
        second_out, second_back = jax.vjp(second_layer, middle_in, second_params, second_table)
        grad_middle, grad_second, grad_second_table = second_back(cot_block * live_three)
        grad_middle = low(grad_middle)
        grad_inputs, grad_first, grad_first_table = first_back(grad_middle)
        carry = jax.tree.map(add_pair, carry, (grad_first, grad_first_table, grad_second, grad_second_table))
        return (carry, (middle_in, low(second_out), grad_inputs, grad_middle))
    start = jax.tree.map(jnp.zeros_like, (first_params, first_table, second_params, second_table))
    totals, results = lax.scan(step, start, (inputs_all, cot_all, live_rows))
    grad_first, grad_first_table, grad_second, grad_second_table = totals
    first_outs, second_outs, first_grads, second_grads = results
    full_shape = (MICRO, IMAGES, TOKIMG, C)
    layer_outputs = jnp.stack([first_outs.reshape(full_shape), second_outs.reshape(full_shape)]).astype(jnp.bfloat16)
    input_grads = jnp.stack([first_grads.reshape(full_shape), second_grads.reshape(full_shape)])
    stacked = tuple((jnp.stack([one_grad, two_grad]) for one_grad, two_grad in zip(grad_first, grad_second)))
    table_grad = jnp.stack([grad_first_table, grad_second_table])
    return (layer_outputs, input_grads, stacked[0], stacked[1], stacked[2], stacked[3], stacked[4], stacked[5], stacked[6], stacked[7], stacked[8], stacked[9], stacked[10], stacked[11], stacked[12], table_grad)
```

```python
import jax
import jax.numpy as jnp
from jax import lax
from jax.experimental import pallas as pl
from jax.experimental.pallas import tpu as pltpu
from jax.sharding import PartitionSpec as P

C = 512
HEADS = 16
HD = 32
FF = 2048
WIN = 7
SIDE = 14
SHIFT = 3
WT = 49
NWIN = 4
TOKIMG = 196
TABLE = 169
EPSILON = 1e-05

PW = 64
ROWS = NWIN * PW
GROUPS = 4
TILES = 12
SCALE = HD ** (-0.5)
F32 = jnp.float32
BF16 = jnp.bfloat16
VMEM_BYTES = 56 * 1024 * 1024


def dot(a, b):
    return jnp.dot(a, b, preferred_element_type=F32)


def dot_nt(a, b):
    return lax.dot_general(a, b, (((1,), (1,)), ((), ())), preferred_element_type=F32)


def dot_tn(a, b):
    return lax.dot_general(a, b, (((0,), (0,)), ((), ())), preferred_element_type=F32)


def normalise(values):
    center = values - jnp.mean(values, -1, keepdims=True)
    rstd = lax.rsqrt(jnp.mean(center * center, -1, keepdims=True) + EPSILON)
    return center * rstd, rstd


def weight_tile(w_ref, c):
    return w_ref[:, c].reshape(C, C)


def down_tile(w_ref, c):
    n = w_ref.shape[0] // 4
    return w_ref[c * n : (c + 1) * n, 8:12].reshape(C, C)


def head_of_lane():
    return lax.broadcasted_iota(jnp.int32, (PW, 128), 1) // HD


def spread_heads(block, lane_head):
    zero = jnp.zeros_like(block)
    return jnp.concatenate([jnp.where(lane_head == h, block, zero) for h in range(4)], 0)


def pick_heads(stack, lane_head):
    out = stack[0:PW]
    for h in range(1, 4):
        out = jnp.where(lane_head == h, stack[h * PW : (h + 1) * PW], out)
    return out


def forward_body(
    x_ref, live_ref, perm_ref, permt_ref, bias_ref, w_ref, vec_ref, pb_ref, ub_ref,
    out_ref, xw_ref, h_ref, qkv_ref, a_ref, r_ref, x1_ref, h2_ref, z_ref, gp_ref,
):
    x = dot(perm_ref[...], x_ref[...])
    xw_ref[...] = x.astype(BF16)
    n1, _ = normalise(x)
    h = (n1 * vec_ref[0:1] + vec_ref[1:2]).astype(BF16)
    h_ref[...] = h
    for c in range(3):
        cols = slice(c * C, (c + 1) * C)
        qkv_ref[:, cols] = (dot(h, weight_tile(w_ref, c)) + pb_ref[:, cols]).astype(BF16)
    lane_head = head_of_lane()
    for w in range(NWIN):
        rows = slice(w * PW, (w + 1) * PW)
        for g in range(GROUPS):
            lanes = g * 128
            q = qkv_ref[rows, lanes : lanes + 128]
            k = qkv_ref[rows, C + lanes : C + lanes + 128]
            v = qkv_ref[rows, 2 * C + lanes : 2 * C + lanes + 128]
            st = dot_nt(k, spread_heads(q, lane_head)) * SCALE + bias_ref[w * GROUPS + g]
            e = jnp.exp(st - jnp.max(st, 0, keepdims=True))
            a = (e * (1.0 / jnp.sum(e, 0, keepdims=True))).astype(BF16)
            a_ref[w * GROUPS + g] = a
            r_ref[rows, lanes : lanes + 128] = pick_heads(dot_tn(a, v), lane_head).astype(BF16)
    x1 = x + (dot(r_ref[...], weight_tile(w_ref, 3)) + vec_ref[2:3])
    x1_ref[...] = x1
    n2, _ = normalise(x1)
    h2 = (n2 * vec_ref[3:4] + vec_ref[4:5]).astype(BF16)
    h2_ref[...] = h2
    total = x1 + vec_ref[5:6]
    for c in range(4):
        cols = slice(c * C, (c + 1) * C)
        g = dot(h2, weight_tile(w_ref, 4 + c)) + ub_ref[:, cols]
        cdf = 0.5 + 0.5 * lax.erf(g * (0.5**0.5))
        pdf = jnp.exp(-0.5 * g * g) * 0.3989422804014327
        z = (g * cdf).astype(BF16)
        z_ref[:, cols] = z
        gp_ref[:, cols] = (cdf + g * pdf).astype(BF16)
        total = total + dot(z, down_tile(w_ref, c))
    out = (total * live_ref[0, 0]).astype(BF16)
    out_ref[...] = dot(permt_ref[...], out).astype(BF16)


def backward_body(
    e_ref, live_ref, perm_ref, permt_ref, w_ref, vec_ref,
    xw_ref, qkv_ref, a_ref, x1_ref, gp_ref,
    dx_ref, sent_ref, do_ref, dg_ref, db_ref, dp_ref, vg_ref, ug_ref, ds_ref,
    dr_ref,
):
    e = dot(perm_ref[...], e_ref[...]) * live_ref[0, 0]
    do = e.astype(BF16)
    do_ref[...] = do
    dh2 = jnp.zeros((ROWS, C), F32)
    for c in range(4):
        cols = slice(c * C, (c + 1) * C)
        dz = dot_nt(do, down_tile(w_ref, c))
        dg = (dz * gp_ref[:, cols].astype(F32)).astype(BF16)
        dg_ref[:, cols] = dg
        ug_ref[:, cols] = jnp.sum(dg.astype(F32), 0, keepdims=True)
        dh2 = dh2 + dot_nt(dg, weight_tile(w_ref, 4 + c))
    n2, r2 = normalise(x1_ref[...])
    d = dh2 * vec_ref[3:4]
    dx1 = e + r2 * (
        d - jnp.mean(d, -1, keepdims=True) - n2 * jnp.mean(d * n2, -1, keepdims=True)
    )
    db = dx1.astype(BF16)
    db_ref[...] = db
    dr_ref[...] = dot_nt(db, weight_tile(w_ref, 3)).astype(BF16)
    lane_head = head_of_lane()
    for w in range(NWIN):
        rows = slice(w * PW, (w + 1) * PW)
        for g in range(GROUPS):
            lanes = g * 128
            q = qkv_ref[rows, lanes : lanes + 128]
            k = qkv_ref[rows, C + lanes : C + lanes + 128]
            v = qkv_ref[rows, 2 * C + lanes : 2 * C + lanes + 128]
            a = a_ref[w * GROUPS + g]
            drs = spread_heads(dr_ref[rows, lanes : lanes + 128], lane_head)
            da = dot_nt(v, drs)
            dv = dot(a, drs)
            af = a.astype(F32)
            pa = da * af
            ds = (pa - af * jnp.sum(pa, 0, keepdims=True)).astype(BF16)
            if w == 0:
                ds_ref[g] = ds.astype(F32)
            else:
                ds_ref[g] += ds.astype(F32)
            dq = pick_heads(dot_tn(ds, k), lane_head) * SCALE
            dk = dot(ds, spread_heads(q, lane_head)) * SCALE
            dp_ref[rows, lanes : lanes + 128] = dq.astype(BF16)
            dp_ref[rows, C + lanes : C + lanes + 128] = dk.astype(BF16)
            dp_ref[rows, 2 * C + lanes : 2 * C + lanes + 128] = dv.astype(BF16)
    dh = jnp.zeros((ROWS, C), F32)
    for c in range(3):
        dh = dh + dot_nt(dp_ref[:, c * C : (c + 1) * C], weight_tile(w_ref, c))
    n1, r1 = normalise(xw_ref[...].astype(F32))
    d = dh * vec_ref[0:1]
    dx = dx1 + r1 * (
        d - jnp.mean(d, -1, keepdims=True) - n1 * jnp.mean(d * n1, -1, keepdims=True)
    )
    high = dx.astype(BF16)
    low = (dx - high.astype(F32)).astype(BF16)
    top = dot(permt_ref[...], high)
    dx_ref[...] = top + dot(permt_ref[...], low)
    sent_ref[...] = top.astype(BF16)

    def column_sum(value):
        return jnp.sum(value.astype(F32), 0, keepdims=True)

    vg_ref[0:1] = column_sum(dh * n1)
    vg_ref[1:2] = column_sum(dh)
    vg_ref[2:3] = column_sum(dp_ref[:, 0:C])
    vg_ref[3:4] = column_sum(dp_ref[:, 2 * C :])
    vg_ref[4:5] = column_sum(db)
    vg_ref[5:6] = column_sum(dh2 * n2)
    vg_ref[6:7] = column_sum(dh2)
    vg_ref[7:8] = column_sum(do)


def weight_grads_body(count, *refs):
    h, r, h2, z, do, dg, db, dp = (refs[i * count : (i + 1) * count] for i in range(8))
    out_ref = refs[8 * count]
    owners = out_ref.shape[0]

    def product(left, lcols, right, rcols):
        total = dot_tn(left[0][:, lcols], right[0][:, rcols])
        for l, r_ in zip(left[1:], right[1:]):
            total = total + dot_tn(l[:, lcols], r_[:, rcols])
        return total.astype(BF16)

    whole = slice(0, C)
    for c in range(3):
        cols = slice(c * C, (c + 1) * C)
        out_ref[:, c] = product(h, whole, dp, cols).reshape(owners, C // owners, C)
    out_ref[:, 3] = product(r, whole, db, whole).reshape(owners, C // owners, C)
    for c in range(4):
        cols = slice(c * C, (c + 1) * C)
        out_ref[:, 4 + c] = product(h2, whole, dg, cols).reshape(owners, C // owners, C)
        n = owners // 4
        out_ref[c * n : (c + 1) * n, 8:12] = product(z, cols, do, whole).reshape(
            n, 4, C // owners, C
        )


def call(body, outs, args, scratch=(), smem=(), flops=0):
    vmem = pl.BlockSpec(memory_space=pltpu.VMEM)
    return pl.pallas_call(
        body,
        out_shape=[jax.ShapeDtypeStruct(s, d) for s, d in outs],
        in_specs=[
            pl.BlockSpec(memory_space=pltpu.SMEM) if i in smem else vmem for i in range(len(args))
        ],
        out_specs=[vmem] * len(outs),
        scratch_shapes=list(scratch),
        compiler_params=pltpu.CompilerParams(vmem_limit_bytes=VMEM_BYTES),
        cost_estimate=pl.CostEstimate(flops=flops, bytes_accessed=16 << 20, transcendentals=0),
    )(*args)


def relative_index():
    position = jnp.arange(WT, dtype=jnp.int32)
    rows_of, cols_of = position // WIN, position % WIN
    return (
        (rows_of[:, None] - rows_of[None, :] + WIN - 1) * (2 * WIN - 1)
        + cols_of[:, None]
        - cols_of[None, :]
        + WIN
        - 1
    )


def token_of_row(is_second):
    row = jnp.arange(ROWS, dtype=jnp.int32)
    window, place = row // PW, row % PW
    shift = jnp.where(is_second, SHIFT, 0)
    r = (window // 2 * WIN + place // WIN + shift) % SIDE
    c = (window % 2 * WIN + place % WIN + shift) % SIDE
    return jnp.where(place < WT, r * SIDE + c, -1)


def pad_pairs(values):
    lead = [(0, 0)] * (values.ndim - 2)
    return jnp.pad(jnp.swapaxes(values, -1, -2), lead + [(0, PW - WT), (0, PW - WT)])


def shards(
    images, counts, shift_mask, cotangent, attention_gain, attention_shift, heads_weight,
    query_bias, value_bias, merge_weight, merge_bias, feed_gain, feed_shift, up_weight, up_bias,
    down_weight, down_bias, bias_table,
):
    owners = lax.axis_size("dp")
    me = lax.axis_index("dp")
    part = C // owners
    is_second = lax.axis_index("section") == 1
    micro = images.shape[0]
    live_rows = (jnp.arange(images.shape[1], dtype=jnp.int32)[None, :] < counts).astype(F32)

    tiles = jnp.concatenate(
        [
            heads_weight[0].reshape(part, 3, C).transpose(1, 0, 2),
            merge_weight[0][None],
            up_weight[0].reshape(part, 4, C).transpose(1, 0, 2),
            down_weight[0].reshape(4, part, C),
        ]
    )
    vector = jnp.concatenate(
        [
            attention_gain[0], attention_shift[0], query_bias[0], value_bias[0], merge_bias[0],
            feed_gain[0], feed_shift[0], down_bias[0], up_bias[0],
        ]
    )
    vectors = lax.all_gather(vector, "dp", axis=0).astype(F32)
    weights = lax.all_gather(tiles, "dp", axis=0)
    wide = vectors[:, : 8 * part].reshape(owners, 8, part).transpose(1, 0, 2).reshape(8, C)
    up_row = vectors[:, 8 * part :].reshape(1, FF)
    vec = wide[jnp.array([0, 1, 4, 5, 6, 7, 7, 7])]
    project_row = jnp.concatenate([wide[2], jnp.zeros_like(wide[2]), wide[3]])[None]

    token = token_of_row(is_second)
    perm = (token[:, None] == jnp.arange(TOKIMG, dtype=jnp.int32)[None, :]).astype(BF16)
    permt = perm.T
    one_hot = (
        relative_index().reshape(-1)[:, None] == jnp.arange(TABLE, dtype=jnp.int32)[None, :]
    ).astype(F32)
    position = jnp.dot(one_hot, bias_table[0].astype(F32), precision=lax.Precision.HIGHEST)
    position = position.reshape(WT, WT, HEADS).transpose(2, 0, 1)
    position = pad_pairs(position).reshape(GROUPS, 4, PW, PW).transpose(0, 2, 1, 3)
    mask = pad_pairs(-100.0 * is_second.astype(F32) * shift_mask.astype(F32))
    edge = jnp.where(jnp.arange(PW) < WT, 0.0, -1e30)[:, None, None]
    bias = position[None] + mask[:, None, :, None, :] + edge
    bias = bias.reshape(NWIN * GROUPS, PW, 4 * PW)

    tick_bf16 = jnp.zeros((TOKIMG, C), BF16)
    received = tick_bf16
    kept, outputs = [], []
    layer_flops = 2 * ROWS * C * C * TILES
    for tick in range(micro + 1):
        own = images[tick, 0] if tick < micro else tick_bf16
        first = live_rows[tick, 0] if tick < micro else 0.0
        second = live_rows[tick - 1, 0] if tick > 0 else 0.0
        live = jnp.where(is_second, second, first).reshape(1, 1)
        source = jnp.where(is_second, received, own)
        out, *stored = call(
            forward_body,
            [
                ((TOKIMG, C), BF16), ((ROWS, C), BF16), ((ROWS, C), BF16), ((ROWS, 3 * C), BF16),
                ((NWIN * GROUPS, PW, 4 * PW), BF16), ((ROWS, C), BF16), ((ROWS, C), F32),
                ((ROWS, C), BF16), ((ROWS, FF), BF16), ((ROWS, FF), BF16),
            ],
            (source, live, perm, permt, bias, weights, vec, project_row, up_row),
            smem=(1,),
            flops=layer_flops,
        )
        kept.append((stored, live))
        outputs.append(out)
        if tick < micro:
            received = lax.ppermute(out, "section", [(0, 1)])
    layer_outputs = jnp.stack(
        [jnp.where(is_second, outputs[m + 1], outputs[m]) for m in range(micro)]
    )[None, :, None]

    received = tick_bf16
    products, grads = [], []
    vec_total = up_total = pair_total = 0.0
    for turn in range(micro + 1):
        (xw, h, qkv, a, r, x1, h2, z, gp), live = kept[micro - turn]
        own = cotangent[micro - 1 - turn, 0] if turn < micro else tick_bf16
        upstream = jnp.where(is_second, own, received)
        dx, sent, do, dg, db, dp, vg, ug, ds = call(
            backward_body,
            [
                ((TOKIMG, C), F32), ((TOKIMG, C), BF16), ((ROWS, C), BF16), ((ROWS, FF), BF16),
                ((ROWS, C), BF16), ((ROWS, 3 * C), BF16), ((8, C), F32), ((1, FF), F32),
                ((GROUPS, PW, 4 * PW), F32),
            ],
            (upstream, live, perm, permt, weights, vec, xw, qkv, a, x1, gp),
            scratch=(pltpu.VMEM((ROWS, C), BF16),),
            smem=(1,),
            flops=layer_flops,
        )
        products.append((h, r, h2, z, do, dg, db, dp))
        vec_total, up_total, pair_total = vec_total + vg, up_total + ug, pair_total + ds
        grads.append(jnp.where(is_second, sent.astype(F32), dx))
        if turn < micro:
            received = lax.ppermute(sent, "section", [(1, 0)])
    input_grads = jnp.stack(
        [
            jnp.where(is_second, grads[micro - 1 - m], grads[micro - m]) for m in range(micro)
        ]
    )[None, :, None]

    count = micro + 1
    (tile_grads,) = call(
        lambda *refs: weight_grads_body(count, *refs),
        [((owners, TILES, part, C), BF16)],
        tuple(p[i] for i in range(8) for p in products),
        flops=layer_flops * count,
    )
    own_tiles = lax.psum_scatter(tile_grads, "dp", scatter_dimension=0, tiled=False).astype(F32)

    pairs = pair_total.reshape(GROUPS, PW, 4, PW)[:, :WT, :, :WT]
    pairs = pairs.transpose(3, 1, 0, 2).reshape(WT * WT, HEADS)
    table = jnp.dot(one_hot.T, pairs, precision=lax.Precision.HIGHEST)
    flat = jnp.concatenate([vec_total.reshape(-1), up_total.reshape(-1), table.reshape(-1)])
    flat = lax.psum(flat, "dp")
    own_vec = lax.dynamic_slice(flat[: 8 * C].reshape(8, C), (0, me * part), (8, part))
    own_up = lax.dynamic_slice(flat[8 * C : 8 * C + FF], (me * (FF // owners),), (FF // owners,))
    table = flat[8 * C + FF :].reshape(1, TABLE, HEADS)
    return (
        layer_outputs,
        input_grads,
        own_vec[0][None],
        own_vec[1][None],
        own_tiles[0:3].transpose(1, 0, 2).reshape(1, part, 3 * C),
        own_vec[2][None],
        own_vec[3][None],
        own_tiles[3][None],
        own_vec[4][None],
        own_vec[5][None],
        own_vec[6][None],
        own_tiles[4:8].transpose(1, 0, 2).reshape(1, part, FF),
        own_up[None],
        own_tiles[8:12].reshape(1, 4 * part, C),
        own_vec[7][None],
        table,
    )


def solution(mesh):
    rows, matrix = P("section", "dp"), P("section", "dp", None)
    tokens = P("section", None, "dp", None, None)
    table = P("section", None, None)
    images = P(None, "dp", None, None)
    return jax.shard_map(
        shards,
        mesh=mesh,
        in_specs=(
            images, P(None, "dp"), P(), images, rows, rows, matrix, rows, rows, matrix, rows,
            rows, rows, matrix, rows, matrix, rows, table,
        ),
        out_specs=(
            tokens, tokens, rows, rows, matrix, rows, rows, matrix, rows, rows, rows, matrix,
            rows, matrix, rows, table,
        ),
        check_vma=False,
    )
```

```python
import jax
import jax.numpy as jnp
from jax import lax
from jax.experimental import pallas as pl
from jax.experimental.pallas import tpu as pltpu
from jax.sharding import PartitionSpec as P

C = 512
HEADS = 16
HD = 32
FF = 2048
WIN = 7
SIDE = 14
SHIFT = 3
WT = 49
NWIN = 4
TOKIMG = 196
TABLE = 169
EPSILON = 1e-05

PW = 64
ROWS = NWIN * PW
GROUPS = 4
TILES = 12
SCALE = HD ** (-0.5)
F32 = jnp.float32
BF16 = jnp.bfloat16
VMEM_BYTES = 56 * 1024 * 1024


def dot(a, b):
    return jnp.dot(a, b, preferred_element_type=F32)


def dot_nt(a, b):
    return lax.dot_general(a, b, (((1,), (1,)), ((), ())), preferred_element_type=F32)


def dot_tn(a, b):
    return lax.dot_general(a, b, (((0,), (0,)), ((), ())), preferred_element_type=F32)


def normalise(values):
    center = values - jnp.mean(values, -1, keepdims=True)
    rstd = lax.rsqrt(jnp.mean(center * center, -1, keepdims=True) + EPSILON)
    return center * rstd, rstd


def weight_tile(w_ref, c):
    return w_ref[:, c].reshape(C, C)


def down_tile(w_ref, c):
    n = w_ref.shape[0] // 4
    return w_ref[c * n : (c + 1) * n, 8:12].reshape(C, C)


def head_of_lane():
    return lax.broadcasted_iota(jnp.int32, (PW, 128), 1) // HD


def spread_heads(block, lane_head):
    zero = jnp.zeros_like(block)
    return jnp.concatenate([jnp.where(lane_head == h, block, zero) for h in range(4)], 0)


def pick_heads(stack, lane_head):
    out = stack[0:PW]
    for h in range(1, 4):
        out = jnp.where(lane_head == h, stack[h * PW : (h + 1) * PW], out)
    return out


def forward_body(
    x_ref, live_ref, perm_ref, permt_ref, bias_ref, w_ref, vec_ref, pb_ref, ub_ref,
    out_ref, xw_ref, h_ref, qkv_ref, a_ref, r_ref, x1_ref, h2_ref, z_ref, gp_ref,
):
    x = dot(perm_ref[...], x_ref[...])
    xw_ref[...] = x.astype(BF16)
    n1, _ = normalise(x)
    h = (n1 * vec_ref[0:1] + vec_ref[1:2]).astype(BF16)
    h_ref[...] = h
    for c in range(3):
        cols = slice(c * C, (c + 1) * C)
        qkv_ref[:, cols] = (dot(h, weight_tile(w_ref, c)) + pb_ref[:, cols]).astype(BF16)
    lane_head = head_of_lane()
    for w in range(NWIN):
        rows = slice(w * PW, (w + 1) * PW)
        for g in range(GROUPS):
            lanes = g * 128
            q = qkv_ref[rows, lanes : lanes + 128]
            k = qkv_ref[rows, C + lanes : C + lanes + 128]
            v = qkv_ref[rows, 2 * C + lanes : 2 * C + lanes + 128]
            st = dot_nt(k, spread_heads(q, lane_head)) * SCALE + bias_ref[w * GROUPS + g]
            e = jnp.exp(st - jnp.max(st, 0, keepdims=True))
            a = (e * (1.0 / jnp.sum(e, 0, keepdims=True))).astype(BF16)
            a_ref[w * GROUPS + g] = a
            r_ref[rows, lanes : lanes + 128] = pick_heads(dot_tn(a, v), lane_head).astype(BF16)
    x1 = x + (dot(r_ref[...], weight_tile(w_ref, 3)) + vec_ref[2:3])
    x1_ref[...] = x1
    n2, _ = normalise(x1)
    h2 = (n2 * vec_ref[3:4] + vec_ref[4:5]).astype(BF16)
    h2_ref[...] = h2
    total = x1 + vec_ref[5:6]
    for c in range(4):
        cols = slice(c * C, (c + 1) * C)
        g = dot(h2, weight_tile(w_ref, 4 + c)) + ub_ref[:, cols]
        cdf = 0.5 + 0.5 * lax.erf(g * (0.5**0.5))
        pdf = jnp.exp(-0.5 * g * g) * 0.3989422804014327
        z = (g * cdf).astype(BF16)
        z_ref[:, cols] = z
        gp_ref[:, cols] = (cdf + g * pdf).astype(BF16)
        total = total + dot(z, down_tile(w_ref, c))
    out = (total * live_ref[0, 0]).astype(BF16)
    out_ref[...] = dot(permt_ref[...], out).astype(BF16)


def backward_body(
    e_ref, live_ref, perm_ref, permt_ref, w_ref, vec_ref,
    xw_ref, qkv_ref, a_ref, x1_ref, gp_ref,
    dx_ref, sent_ref, do_ref, dg_ref, db_ref, dp_ref, vg_ref, ug_ref, ds_ref,
    dr_ref,
):
    e = dot(perm_ref[...], e_ref[...]) * live_ref[0, 0]
    do = e.astype(BF16)
    do_ref[...] = do
    dh2 = jnp.zeros((ROWS, C), F32)
    for c in range(4):
        cols = slice(c * C, (c + 1) * C)
        dz = dot_nt(do, down_tile(w_ref, c))
        dg = (dz * gp_ref[:, cols].astype(F32)).astype(BF16)
        dg_ref[:, cols] = dg
        ug_ref[:, cols] = jnp.sum(dg.astype(F32), 0, keepdims=True)
        dh2 = dh2 + dot_nt(dg, weight_tile(w_ref, 4 + c))
    n2, r2 = normalise(x1_ref[...])
    d = dh2 * vec_ref[3:4]
    dx1 = e + r2 * (
        d - jnp.mean(d, -1, keepdims=True) - n2 * jnp.mean(d * n2, -1, keepdims=True)
    )
    db = dx1.astype(BF16)
    db_ref[...] = db
    dr_ref[...] = dot_nt(db, weight_tile(w_ref, 3)).astype(BF16)
    lane_head = head_of_lane()
    for w in range(NWIN):
        rows = slice(w * PW, (w + 1) * PW)
        for g in range(GROUPS):
            lanes = g * 128
            q = qkv_ref[rows, lanes : lanes + 128]
            k = qkv_ref[rows, C + lanes : C + lanes + 128]
            v = qkv_ref[rows, 2 * C + lanes : 2 * C + lanes + 128]
            a = a_ref[w * GROUPS + g]
            drs = spread_heads(dr_ref[rows, lanes : lanes + 128], lane_head)
            da = dot_nt(v, drs)
            dv = dot(a, drs)
            af = a.astype(F32)
            pa = da * af
            ds = (pa - af * jnp.sum(pa, 0, keepdims=True)).astype(BF16)
            if w == 0:
                ds_ref[g] = ds.astype(F32)
            else:
                ds_ref[g] += ds.astype(F32)
            dq = pick_heads(dot_tn(ds, k), lane_head) * SCALE
            dk = dot(ds, spread_heads(q, lane_head)) * SCALE
            dp_ref[rows, lanes : lanes + 128] = dq.astype(BF16)
            dp_ref[rows, C + lanes : C + lanes + 128] = dk.astype(BF16)
            dp_ref[rows, 2 * C + lanes : 2 * C + lanes + 128] = dv.astype(BF16)
    dh = jnp.zeros((ROWS, C), F32)
    for c in range(3):
        dh = dh + dot_nt(dp_ref[:, c * C : (c + 1) * C], weight_tile(w_ref, c))
    n1, r1 = normalise(xw_ref[...].astype(F32))
    d = dh * vec_ref[0:1]
    dx = dx1 + r1 * (
        d - jnp.mean(d, -1, keepdims=True) - n1 * jnp.mean(d * n1, -1, keepdims=True)
    )
    high = dx.astype(BF16)
    low = (dx - high.astype(F32)).astype(BF16)
    top = dot(permt_ref[...], high)
    dx_ref[...] = top + dot(permt_ref[...], low)
    sent_ref[...] = top.astype(BF16)

    def column_sum(value):
        return jnp.sum(value.astype(F32), 0, keepdims=True)

    vg_ref[0:1] = column_sum(dh * n1)
    vg_ref[1:2] = column_sum(dh)
    vg_ref[2:3] = column_sum(dp_ref[:, 0:C])
    vg_ref[3:4] = column_sum(dp_ref[:, 2 * C :])
    vg_ref[4:5] = column_sum(db)
    vg_ref[5:6] = column_sum(dh2 * n2)
    vg_ref[6:7] = column_sum(dh2)
    vg_ref[7:8] = column_sum(do)


def weight_grads_body(count, *refs):
    h, r, h2, z, do, dg, db, dp = (refs[i * count : (i + 1) * count] for i in range(8))
    extra_ref, out_ref = refs[8 * count :]
    out_ref[:, TILES:] = extra_ref[...]
    owners = out_ref.shape[0]

    def product(left, lcols, right, rcols):
        total = dot_tn(left[0][:, lcols], right[0][:, rcols])
        for l, r_ in zip(left[1:], right[1:]):
            total = total + dot_tn(l[:, lcols], r_[:, rcols])
        return total.astype(BF16)

    whole = slice(0, C)
    for c in range(3):
        cols = slice(c * C, (c + 1) * C)
        out_ref[:, c] = product(h, whole, dp, cols).reshape(owners, C // owners, C)
    out_ref[:, 3] = product(r, whole, db, whole).reshape(owners, C // owners, C)
    for c in range(4):
        cols = slice(c * C, (c + 1) * C)
        out_ref[:, 4 + c] = product(h2, whole, dg, cols).reshape(owners, C // owners, C)
        n = owners // 4
        out_ref[c * n : (c + 1) * n, 8:12] = product(z, cols, do, whole).reshape(
            n, 4, C // owners, C
        )


def scatter_body(g_ref, out_ref, ra, rb, sa, sb, ra2, rb2, total, rz, send, recv):
    section, me = lax.axis_index("section"), lax.axis_index("dp")
    z, y, x = me // 4, me // 2 % 2, me % 2
    half = ra.shape[2]
    y_peer, x_peer = z * 4 + (1 - y) * 2 + x, z * 4 + y * 2 + (1 - x)
    z_peers = [((z + k) % 4) * 4 + y * 2 + x for k in (1, 2, 3)]
    barrier = pltpu.get_barrier_semaphore()
    for peer in [y_peer, x_peer] + z_peers:
        pl.semaphore_signal(
            barrier, inc=1, device_id=(section, peer), device_id_type=pl.DeviceIdType.MESH
        )
    pl.semaphore_wait(barrier, 5)

    def send_to(source, target, slot, peer):
        copy = pltpu.make_async_remote_copy(
            src_ref=source,
            dst_ref=target,
            send_sem=send.at[slot],
            recv_sem=recv.at[slot],
            device_id=(section, peer),
            device_id_type=pl.DeviceIdType.MESH,
        )
        copy.start()
        return copy

    def add(a, b):
        return (a.astype(F32) + b.astype(F32)).astype(BF16)

    first_a = send_to(g_ref.at[:, 1 - y, :, 0:half], ra, 0, y_peer)
    first_b = send_to(g_ref.at[:, :, 1 - x, half:], rb, 1, x_peer)
    first_a.wait()

    @pl.loop(0, 4)
    def _(i):
        sa[i] = add(g_ref[i, y, :, 0:half], ra[i])

    second_a = send_to(sa.at[:, 1 - x], ra2, 2, x_peer)
    first_b.wait()

    @pl.loop(0, 4)
    def _(i):
        sb[i] = add(g_ref[i, :, x, half:], rb[i])

    second_b = send_to(sb.at[:, 1 - y], rb2, 3, y_peer)
    second_a.wait()
    second_b.wait()

    @pl.loop(0, 4)
    def _(i):
        total[i, 0:half] = add(sa[i, x], ra2[i])
        total[i, half:] = add(sb[i, y], rb2[i])

    last = [
        send_to(total.at[(z + k) % 4], rz.at[k - 1], 3 + k, z_peers[k - 1]) for k in (1, 2, 3)
    ]
    for copy in last:
        copy.wait()
    out_ref[...] = (total[z].astype(F32) + rz[0].astype(F32)) + (
        rz[1].astype(F32) + rz[2].astype(F32)
    )


def scatter_sum(value, grid_ok):
    owners, tiles, part, width = value.shape
    if not grid_ok:
        return lax.psum_scatter(value, "dp", scatter_dimension=0, tiled=False).astype(F32)
    half = (tiles + 1) // 2
    rest = tiles - half

    def buffer(*lead):
        return pltpu.VMEM((*lead, part, width), BF16)

    vmem = pl.BlockSpec(memory_space=pltpu.VMEM)
    return pl.pallas_call(
        scatter_body,
        out_shape=jax.ShapeDtypeStruct((tiles, part, width), F32),
        in_specs=[vmem],
        out_specs=vmem,
        scratch_shapes=[
            buffer(4, 2, half), buffer(4, 2, rest), buffer(4, 2, half), buffer(4, 2, rest),
            buffer(4, half), buffer(4, rest), buffer(4, tiles), buffer(3, tiles),
            pltpu.SemaphoreType.DMA((7,)), pltpu.SemaphoreType.DMA((7,)),
        ],
        compiler_params=pltpu.CompilerParams(
            collective_id=0, has_side_effects=True, vmem_limit_bytes=VMEM_BYTES
        ),
    )(value.reshape(4, 2, 2, tiles, part, width))


def call(body, outs, args, scratch=(), smem=(), flops=0):
    vmem = pl.BlockSpec(memory_space=pltpu.VMEM)
    return pl.pallas_call(
        body,
        out_shape=[jax.ShapeDtypeStruct(s, d) for s, d in outs],
        in_specs=[
            pl.BlockSpec(memory_space=pltpu.SMEM) if i in smem else vmem for i in range(len(args))
        ],
        out_specs=[vmem] * len(outs),
        scratch_shapes=list(scratch),
        compiler_params=pltpu.CompilerParams(vmem_limit_bytes=VMEM_BYTES),
        cost_estimate=pl.CostEstimate(flops=flops, bytes_accessed=16 << 20, transcendentals=0),
    )(*args)


def relative_index():
    position = jnp.arange(WT, dtype=jnp.int32)
    rows_of, cols_of = position // WIN, position % WIN
    return (
        (rows_of[:, None] - rows_of[None, :] + WIN - 1) * (2 * WIN - 1)
        + cols_of[:, None]
        - cols_of[None, :]
        + WIN
        - 1
    )


def token_of_row(is_second):
    row = jnp.arange(ROWS, dtype=jnp.int32)
    window, place = row // PW, row % PW
    shift = jnp.where(is_second, SHIFT, 0)
    r = (window // 2 * WIN + place // WIN + shift) % SIDE
    c = (window % 2 * WIN + place % WIN + shift) % SIDE
    return jnp.where(place < WT, r * SIDE + c, -1)


def pad_pairs(values):
    lead = [(0, 0)] * (values.ndim - 2)
    return jnp.pad(jnp.swapaxes(values, -1, -2), lead + [(0, PW - WT), (0, PW - WT)])


def shards(
    images, counts, shift_mask, cotangent, attention_gain, attention_shift, heads_weight,
    query_bias, value_bias, merge_weight, merge_bias, feed_gain, feed_shift, up_weight, up_bias,
    down_weight, down_bias, bias_table,
):
    owners = lax.axis_size("dp")
    grid_ok = owners == 16
    part = C // owners
    is_second = lax.axis_index("section") == 1
    micro = images.shape[0]
    live_rows = (jnp.arange(images.shape[1], dtype=jnp.int32)[None, :] < counts).astype(F32)

    tiles = jnp.concatenate(
        [
            heads_weight[0].reshape(part, 3, C).transpose(1, 0, 2),
            merge_weight[0][None],
            up_weight[0].reshape(part, 4, C).transpose(1, 0, 2),
            down_weight[0].reshape(4, part, C),
        ]
    )
    own_up_size = FF // owners
    vector = jnp.concatenate(
        [
            attention_gain[0], attention_shift[0], query_bias[0], value_bias[0], merge_bias[0],
            feed_gain[0], feed_shift[0], down_bias[0], up_bias[0],
        ]
    )
    vector = jnp.pad(vector, (0, part * C - vector.size)).reshape(1, part, C)
    weights = lax.all_gather(jnp.concatenate([tiles, vector]), "dp", axis=0)
    vectors = weights[:, TILES].reshape(owners, part * C)[:, : 8 * part + own_up_size].astype(F32)
    wide = vectors[:, : 8 * part].reshape(owners, 8, part).transpose(1, 0, 2).reshape(8, C)
    up_row = vectors[:, 8 * part :].reshape(1, FF)
    vec = wide[jnp.array([0, 1, 4, 5, 6, 7, 7, 7])]
    project_row = jnp.concatenate([wide[2], jnp.zeros_like(wide[2]), wide[3]])[None]

    token = token_of_row(is_second)
    perm = (token[:, None] == jnp.arange(TOKIMG, dtype=jnp.int32)[None, :]).astype(BF16)
    permt = perm.T
    one_hot = (
        relative_index().reshape(-1)[:, None] == jnp.arange(TABLE, dtype=jnp.int32)[None, :]
    ).astype(F32)
    position = jnp.dot(one_hot, bias_table[0].astype(F32), precision=lax.Precision.HIGHEST)
    position = position.reshape(WT, WT, HEADS).transpose(2, 0, 1)
    position = pad_pairs(position).reshape(GROUPS, 4, PW, PW).transpose(0, 2, 1, 3)
    mask = pad_pairs(-100.0 * is_second.astype(F32) * shift_mask.astype(F32))
    edge = jnp.where(jnp.arange(PW) < WT, 0.0, -1e30)[:, None, None]
    bias = position[None] + mask[:, None, :, None, :] + edge
    bias = bias.reshape(NWIN * GROUPS, PW, 4 * PW)

    tick_bf16 = jnp.zeros((TOKIMG, C), BF16)
    received = tick_bf16
    kept, outputs = [], []
    layer_flops = 2 * ROWS * C * C * TILES
    for tick in range(micro + 1):
        own = images[tick, 0] if tick < micro else tick_bf16
        first = live_rows[tick, 0] if tick < micro else 0.0
        second = live_rows[tick - 1, 0] if tick > 0 else 0.0
        live = jnp.where(is_second, second, first).reshape(1, 1)
        source = jnp.where(is_second, received, own)
        out, *stored = call(
            forward_body,
            [
                ((TOKIMG, C), BF16), ((ROWS, C), BF16), ((ROWS, C), BF16), ((ROWS, 3 * C), BF16),
                ((NWIN * GROUPS, PW, 4 * PW), BF16), ((ROWS, C), BF16), ((ROWS, C), F32),
                ((ROWS, C), BF16), ((ROWS, FF), BF16), ((ROWS, FF), BF16),
            ],
            (source, live, perm, permt, bias, weights, vec, project_row, up_row),
            smem=(1,),
            flops=layer_flops,
        )
        kept.append((stored, live))
        outputs.append(out)
        if tick < micro:
            received = lax.ppermute(out, "section", [(0, 1)])
    layer_outputs = jnp.stack(
        [jnp.where(is_second, outputs[m + 1], outputs[m]) for m in range(micro)]
    )[None, :, None]

    received = tick_bf16
    products, grads = [], []
    vec_total = up_total = pair_total = 0.0
    for turn in range(micro + 1):
        (xw, h, qkv, a, r, x1, h2, z, gp), live = kept[micro - turn]
        own = cotangent[micro - 1 - turn, 0] if turn < micro else tick_bf16
        upstream = jnp.where(is_second, own, received)
        dx, sent, do, dg, db, dp, vg, ug, ds = call(
            backward_body,
            [
                ((TOKIMG, C), F32), ((TOKIMG, C), BF16), ((ROWS, C), BF16), ((ROWS, FF), BF16),
                ((ROWS, C), BF16), ((ROWS, 3 * C), BF16), ((8, C), F32), ((1, FF), F32),
                ((GROUPS, PW, 4 * PW), F32),
            ],
            (upstream, live, perm, permt, weights, vec, xw, qkv, a, x1, gp),
            scratch=(pltpu.VMEM((ROWS, C), BF16),),
            smem=(1,),
            flops=layer_flops,
        )
        products.append((h, r, h2, z, do, dg, db, dp))
        vec_total, up_total, pair_total = vec_total + vg, up_total + ug, pair_total + ds
        grads.append(jnp.where(is_second, sent.astype(F32), dx))
        if turn < micro:
            received = lax.ppermute(sent, "section", [(1, 0)])
    input_grads = jnp.stack(
        [
            jnp.where(is_second, grads[micro - 1 - m], grads[micro - m]) for m in range(micro)
        ]
    )[None, :, None]

    count = micro + 1
    pairs = pair_total.reshape(GROUPS, PW, 4, PW)[:, :WT, :, :WT]
    pairs = pairs.transpose(3, 1, 0, 2).reshape(WT * WT, HEADS)
    table = jnp.dot(one_hot.T, pairs, precision=lax.Precision.HIGHEST).reshape(1, -1)
    extra = jnp.concatenate(
        [
            vec_total.reshape(8, owners, part).transpose(1, 0, 2).reshape(owners, 8 * part),
            up_total.reshape(owners, own_up_size),
            jnp.broadcast_to(table, (owners, table.size)),
        ],
        1,
    ).astype(BF16)
    more = -(-extra.shape[1] // (part * C))
    extra = jnp.pad(extra, ((0, 0), (0, more * part * C - extra.shape[1])))
    extra = extra.reshape(owners, more, part, C)
    (tile_grads,) = call(
        lambda *refs: weight_grads_body(count, *refs),
        [((owners, TILES + more, part, C), BF16)],
        tuple(p[i] for i in range(8) for p in products) + (extra,),
        flops=layer_flops * count,
    )
    own_tiles = scatter_sum(tile_grads, grid_ok)
    flat = own_tiles[TILES:].reshape(-1)
    own_vec = flat[: 8 * part].reshape(8, part)
    own_up = flat[8 * part : 8 * part + own_up_size]
    start = 8 * part + own_up_size
    table = flat[start : start + TABLE * HEADS].reshape(1, TABLE, HEADS)
    return (
        layer_outputs,
        input_grads,
        own_vec[0][None],
        own_vec[1][None],
        own_tiles[0:3].transpose(1, 0, 2).reshape(1, part, 3 * C),
        own_vec[2][None],
        own_vec[3][None],
        own_tiles[3][None],
        own_vec[4][None],
        own_vec[5][None],
        own_vec[6][None],
        own_tiles[4:8].transpose(1, 0, 2).reshape(1, part, FF),
        own_up[None],
        own_tiles[8:12].reshape(1, 4 * part, C),
        own_vec[7][None],
        table,
    )


def solution(mesh):
    rows, matrix = P("section", "dp"), P("section", "dp", None)
    tokens = P("section", None, "dp", None, None)
    table = P("section", None, None)
    images = P(None, "dp", None, None)
    return jax.shard_map(
        shards,
        mesh=mesh,
        in_specs=(
            images, P(None, "dp"), P(), images, rows, rows, matrix, rows, rows, matrix, rows,
            rows, rows, matrix, rows, matrix, rows, table,
        ),
        out_specs=(
            tokens, tokens, rows, rows, matrix, rows, rows, matrix, rows, rows, rows, matrix,
            rows, matrix, rows, table,
        ),
        check_vma=False,
    )
```

```python
import jax
import jax.numpy as jnp
from jax import lax
from jax.experimental import pallas as pl
from jax.experimental.pallas import tpu as pltpu
from jax.sharding import PartitionSpec as P

C = 512
HEADS = 16
HD = 32
FF = 2048
WIN = 7
SIDE = 14
SHIFT = 3
WT = 49
NWIN = 4
TOKIMG = 196
TABLE = 169
EPSILON = 1e-05

PW = 64
ROWS = NWIN * PW
GROUPS = 4
TILES = 12
SCALE = HD ** (-0.5)
F32 = jnp.float32
BF16 = jnp.bfloat16
VMEM_BYTES = 56 * 1024 * 1024


def dot(a, b):
    return jnp.dot(a, b, preferred_element_type=F32)


def dot_nt(a, b):
    return lax.dot_general(a, b, (((1,), (1,)), ((), ())), preferred_element_type=F32)


def dot_tn(a, b):
    return lax.dot_general(a, b, (((0,), (0,)), ((), ())), preferred_element_type=F32)


def normalise(values):
    center = values - jnp.mean(values, -1, keepdims=True)
    rstd = lax.rsqrt(jnp.mean(center * center, -1, keepdims=True) + EPSILON)
    return center * rstd, rstd


def weight_tile(w_ref, c):
    return w_ref[:, c].reshape(C, C)


def down_tile(w_ref, c):
    n = w_ref.shape[0] // 4
    return w_ref[c * n : (c + 1) * n, 8:12].reshape(C, C)


def head_of_lane():
    return lax.broadcasted_iota(jnp.int32, (PW, 128), 1) // HD


def spread_heads(block, lane_head):
    zero = jnp.zeros_like(block)
    return jnp.concatenate([jnp.where(lane_head == h, block, zero) for h in range(4)], 0)


def pick_heads(stack, lane_head):
    out = stack[0:PW]
    for h in range(1, 4):
        out = jnp.where(lane_head == h, stack[h * PW : (h + 1) * PW], out)
    return out


def forward_body(
    x_ref, live_ref, perm_ref, permt_ref, bias_ref, w_ref, vec_ref, pb_ref, ub_ref,
    out_ref, xw_ref, h_ref, qkv_ref, a_ref, r_ref, x1_ref, h2_ref, z_ref, gp_ref,
):
    x = dot(perm_ref[...], x_ref[...])
    xw_ref[...] = x.astype(BF16)
    n1, _ = normalise(x)
    h = (n1 * vec_ref[0:1] + vec_ref[1:2]).astype(BF16)
    h_ref[...] = h
    for c in range(3):
        cols = slice(c * C, (c + 1) * C)
        qkv_ref[:, cols] = (dot(h, weight_tile(w_ref, c)) + pb_ref[:, cols]).astype(BF16)
    lane_head = head_of_lane()
    for w in range(NWIN):
        rows = slice(w * PW, (w + 1) * PW)
        for g in range(GROUPS):
            lanes = g * 128
            q = qkv_ref[rows, lanes : lanes + 128]
            k = qkv_ref[rows, C + lanes : C + lanes + 128]
            v = qkv_ref[rows, 2 * C + lanes : 2 * C + lanes + 128]
            st = dot_nt(k, spread_heads(q, lane_head)) * SCALE + bias_ref[w * GROUPS + g]
            e = jnp.exp(st - jnp.max(st, 0, keepdims=True))
            a = (e * (1.0 / jnp.sum(e, 0, keepdims=True))).astype(BF16)
            a_ref[w * GROUPS + g] = a
            r_ref[rows, lanes : lanes + 128] = pick_heads(dot_tn(a, v), lane_head).astype(BF16)
    x1 = x + (dot(r_ref[...], weight_tile(w_ref, 3)) + vec_ref[2:3])
    x1_ref[...] = x1
    n2, _ = normalise(x1)
    h2 = (n2 * vec_ref[3:4] + vec_ref[4:5]).astype(BF16)
    h2_ref[...] = h2
    total = x1 + vec_ref[5:6]
    for c in range(4):
        cols = slice(c * C, (c + 1) * C)
        g = dot(h2, weight_tile(w_ref, 4 + c)) + ub_ref[:, cols]
        cdf = 0.5 + 0.5 * lax.erf(g * (0.5**0.5))
        pdf = jnp.exp(-0.5 * g * g) * 0.3989422804014327
        z = (g * cdf).astype(BF16)
        z_ref[:, cols] = z
        gp_ref[:, cols] = (cdf + g * pdf).astype(BF16)
        total = total + dot(z, down_tile(w_ref, c))
    out = (total * live_ref[0, 0]).astype(BF16)
    out_ref[...] = dot(permt_ref[...], out).astype(BF16)


def backward_body(
    e_ref, live_ref, perm_ref, permt_ref, w_ref, vec_ref,
    xw_ref, qkv_ref, a_ref, x1_ref, gp_ref,
    dx_ref, sent_ref, do_ref, dg_ref, db_ref, dp_ref, vg_ref, ug_ref, ds_ref,
    dr_ref,
):
    e = dot(perm_ref[...], e_ref[...]) * live_ref[0, 0]
    do = e.astype(BF16)
    do_ref[...] = do
    dh2 = jnp.zeros((ROWS, C), F32)
    for c in range(4):
        cols = slice(c * C, (c + 1) * C)
        dz = dot_nt(do, down_tile(w_ref, c))
        dg = (dz * gp_ref[:, cols].astype(F32)).astype(BF16)
        dg_ref[:, cols] = dg
        ug_ref[:, cols] = jnp.sum(dg.astype(F32), 0, keepdims=True)
        dh2 = dh2 + dot_nt(dg, weight_tile(w_ref, 4 + c))
    n2, r2 = normalise(x1_ref[...])
    d = dh2 * vec_ref[3:4]
    dx1 = e + r2 * (
        d - jnp.mean(d, -1, keepdims=True) - n2 * jnp.mean(d * n2, -1, keepdims=True)
    )
    db = dx1.astype(BF16)
    db_ref[...] = db
    dr_ref[...] = dot_nt(db, weight_tile(w_ref, 3)).astype(BF16)
    lane_head = head_of_lane()
    for w in range(NWIN):
        rows = slice(w * PW, (w + 1) * PW)
        for g in range(GROUPS):
            lanes = g * 128
            q = qkv_ref[rows, lanes : lanes + 128]
            k = qkv_ref[rows, C + lanes : C + lanes + 128]
            v = qkv_ref[rows, 2 * C + lanes : 2 * C + lanes + 128]
            a = a_ref[w * GROUPS + g]
            drs = spread_heads(dr_ref[rows, lanes : lanes + 128], lane_head)
            da = dot_nt(v, drs)
            dv = dot(a, drs)
            af = a.astype(F32)
            pa = da * af
            ds = (pa - af * jnp.sum(pa, 0, keepdims=True)).astype(BF16)
            if w == 0:
                ds_ref[g] = ds.astype(F32)
            else:
                ds_ref[g] += ds.astype(F32)
            dq = pick_heads(dot_tn(ds, k), lane_head) * SCALE
            dk = dot(ds, spread_heads(q, lane_head)) * SCALE
            dp_ref[rows, lanes : lanes + 128] = dq.astype(BF16)
            dp_ref[rows, C + lanes : C + lanes + 128] = dk.astype(BF16)
            dp_ref[rows, 2 * C + lanes : 2 * C + lanes + 128] = dv.astype(BF16)
    dh = jnp.zeros((ROWS, C), F32)
    for c in range(3):
        dh = dh + dot_nt(dp_ref[:, c * C : (c + 1) * C], weight_tile(w_ref, c))
    n1, r1 = normalise(xw_ref[...].astype(F32))
    d = dh * vec_ref[0:1]
    dx = dx1 + r1 * (
        d - jnp.mean(d, -1, keepdims=True) - n1 * jnp.mean(d * n1, -1, keepdims=True)
    )
    high = dx.astype(BF16)
    low = (dx - high.astype(F32)).astype(BF16)
    top = dot(permt_ref[...], high)
    dx_ref[...] = top + dot(permt_ref[...], low)
    sent_ref[...] = top.astype(BF16)

    def column_sum(value):
        return jnp.sum(value.astype(F32), 0, keepdims=True)

    vg_ref[0:1] = column_sum(dh * n1)
    vg_ref[1:2] = column_sum(dh)
    vg_ref[2:3] = column_sum(dp_ref[:, 0:C])
    vg_ref[3:4] = column_sum(dp_ref[:, 2 * C :])
    vg_ref[4:5] = column_sum(db)
    vg_ref[5:6] = column_sum(dh2 * n2)
    vg_ref[6:7] = column_sum(dh2)
    vg_ref[7:8] = column_sum(do)


def weight_grads_body(count, *refs):
    h, r, h2, z, do, dg, db, dp = (refs[i * count : (i + 1) * count] for i in range(8))
    extra_ref, out_ref = refs[8 * count :]
    out_ref[:, TILES:] = extra_ref[...]
    owners = out_ref.shape[0]

    def product(left, lcols, right, rcols):
        total = dot_tn(left[0][:, lcols], right[0][:, rcols])
        for l, r_ in zip(left[1:], right[1:]):
            total = total + dot_tn(l[:, lcols], r_[:, rcols])
        return total.astype(BF16)

    whole = slice(0, C)
    for c in range(3):
        cols = slice(c * C, (c + 1) * C)
        out_ref[:, c] = product(h, whole, dp, cols).reshape(owners, C // owners, C)
    out_ref[:, 3] = product(r, whole, db, whole).reshape(owners, C // owners, C)
    for c in range(4):
        cols = slice(c * C, (c + 1) * C)
        out_ref[:, 4 + c] = product(h2, whole, dg, cols).reshape(owners, C // owners, C)
        n = owners // 4
        out_ref[c * n : (c + 1) * n, 8:12] = product(z, cols, do, whole).reshape(
            n, 4, C // owners, C
        )


def block_peers():
    section, me = lax.axis_index("section"), lax.axis_index("dp")
    z, y, x = me // 4, me // 2 % 2, me % 2
    y_peer, x_peer = z * 4 + (1 - y) * 2 + x, z * 4 + y * 2 + (1 - x)
    z_peers = [((z + k) % 4) * 4 + y * 2 + x for k in (1, 2, 3)]
    barrier = pltpu.get_barrier_semaphore()
    for peer in [y_peer, x_peer] + z_peers:
        pl.semaphore_signal(
            barrier, inc=1, device_id=(section, peer), device_id_type=pl.DeviceIdType.MESH
        )
    pl.semaphore_wait(barrier, 5)
    return section, z, y, x, y_peer, x_peer, z_peers


def sender(section, send, recv):
    def send_to(source, target, slot, peer):
        copy = pltpu.make_async_remote_copy(
            src_ref=source,
            dst_ref=target,
            send_sem=send.at[slot],
            recv_sem=recv.at[slot],
            device_id=(section, peer),
            device_id_type=pl.DeviceIdType.MESH,
        )
        copy.start()
        return copy

    return send_to


def gather_body(own_ref, out_ref, send, recv):
    section, z, y, x, y_peer, x_peer, z_peers = block_peers()
    send_to = sender(section, send, recv)
    half = (own_ref.shape[0] + 1) // 2
    along = {
        k: send_to(own_ref, out_ref.at[z, y, x], k - 1, z_peers[k - 1]) for k in (1, 3, 2)
    }
    out_ref[z, y, x] = own_ref[...]
    second, third = {}, []

    def forward_pair(k):
        plane = (z + 4 - k) % 4
        for copy in second[k]:
            copy.wait()
        rows = out_ref.at[plane, y, :, 0:half]
        third.append(send_to(rows, rows, 11 + k, y_peer))
        cols = out_ref.at[plane, :, x, half:]
        third.append(send_to(cols, cols, 15 + k, x_peer))

    order = (0, 1, 3, 2)
    for i, k in enumerate(order):
        plane = (z + 4 - k) % 4
        if k:
            along[k].wait()
        low, high = out_ref.at[plane, y, x, 0:half], out_ref.at[plane, y, x, half:]
        second[k] = (send_to(low, low, 3 + k, x_peer), send_to(high, high, 7 + k, y_peer))
        if i:
            forward_pair(order[i - 1])
    forward_pair(order[-1])
    for copy in third:
        copy.wait()


def gather(value, grid_ok):
    if not grid_ok:
        return lax.all_gather(value, "dp", axis=0)
    vmem = pl.BlockSpec(memory_space=pltpu.VMEM)
    out = pl.pallas_call(
        gather_body,
        out_shape=jax.ShapeDtypeStruct((4, 2, 2, *value.shape), value.dtype),
        in_specs=[vmem],
        out_specs=vmem,
        scratch_shapes=[pltpu.SemaphoreType.DMA((19,)), pltpu.SemaphoreType.DMA((19,))],
        compiler_params=pltpu.CompilerParams(
            collective_id=1, has_side_effects=True, vmem_limit_bytes=VMEM_BYTES
        ),
    )(value)
    return out.reshape(16, *value.shape)


def scatter_body(g_ref, out_ref, ra, rb, sa, sb, ra2, rb2, total, rz, send, recv):
    section, z, y, x, y_peer, x_peer, z_peers = block_peers()
    send_to = sender(section, send, recv)
    half = ra.shape[2]

    def add(a, b):
        return (a.astype(F32) + b.astype(F32)).astype(BF16)

    first, second, last = {}, {}, []
    order = (2, 1, 3, 0)

    def start(k):
        plane = (z + k) % 4
        first[k] = (
            send_to(g_ref.at[plane, 1 - y, :, 0:half], ra.at[k], k, y_peer),
            send_to(g_ref.at[plane, :, 1 - x, half:], rb.at[k], 4 + k, x_peer),
        )

    def middle(k):
        plane = (z + k) % 4
        first[k][0].wait()
        sa[k] = add(g_ref[plane, y, :, 0:half], ra[k])
        copy = send_to(sa.at[k, 1 - x], ra2.at[k], 8 + k, x_peer)
        first[k][1].wait()
        sb[k] = add(g_ref[plane, :, x, half:], rb[k])
        second[k] = (copy, send_to(sb.at[k, 1 - y], rb2.at[k], 12 + k, y_peer))

    def finish(k):
        for copy in second[k]:
            copy.wait()
        total[k, 0:half] = add(sa[k, x], ra2[k])
        total[k, half:] = add(sb[k, y], rb2[k])
        if k:
            last.append(send_to(total.at[k], rz.at[k - 1], 15 + k, z_peers[k - 1]))

    start(order[0])
    start(order[1])
    for i, k in enumerate(order):
        middle(k)
        if i + 2 < 4:
            start(order[i + 2])
        if i:
            finish(order[i - 1])
    finish(order[-1])
    for copy in last:
        copy.wait()
    out_ref[...] = (total[0].astype(F32) + rz[0].astype(F32)) + (
        rz[1].astype(F32) + rz[2].astype(F32)
    )


def scatter_sum(value, grid_ok):
    owners, tiles, part, width = value.shape
    if not grid_ok:
        return lax.psum_scatter(value, "dp", scatter_dimension=0, tiled=False).astype(F32)
    half = (tiles + 1) // 2
    rest = tiles - half

    def buffer(*lead):
        return pltpu.VMEM((*lead, part, width), BF16)

    vmem = pl.BlockSpec(memory_space=pltpu.VMEM)
    return pl.pallas_call(
        scatter_body,
        out_shape=jax.ShapeDtypeStruct((tiles, part, width), F32),
        in_specs=[vmem],
        out_specs=vmem,
        scratch_shapes=[
            buffer(4, 2, half), buffer(4, 2, rest), buffer(4, 2, half), buffer(4, 2, rest),
            buffer(4, half), buffer(4, rest), buffer(4, tiles), buffer(3, tiles),
            pltpu.SemaphoreType.DMA((19,)), pltpu.SemaphoreType.DMA((19,)),
        ],
        compiler_params=pltpu.CompilerParams(
            collective_id=0, has_side_effects=True, vmem_limit_bytes=VMEM_BYTES
        ),
    )(value.reshape(4, 2, 2, tiles, part, width))


def call(body, outs, args, scratch=(), smem=(), flops=0):
    vmem = pl.BlockSpec(memory_space=pltpu.VMEM)
    return pl.pallas_call(
        body,
        out_shape=[jax.ShapeDtypeStruct(s, d) for s, d in outs],
        in_specs=[
            pl.BlockSpec(memory_space=pltpu.SMEM) if i in smem else vmem for i in range(len(args))
        ],
        out_specs=[vmem] * len(outs),
        scratch_shapes=list(scratch),
        compiler_params=pltpu.CompilerParams(vmem_limit_bytes=VMEM_BYTES),
        cost_estimate=pl.CostEstimate(flops=flops, bytes_accessed=16 << 20, transcendentals=0),
    )(*args)


def relative_index():
    position = jnp.arange(WT, dtype=jnp.int32)
    rows_of, cols_of = position // WIN, position % WIN
    return (
        (rows_of[:, None] - rows_of[None, :] + WIN - 1) * (2 * WIN - 1)
        + cols_of[:, None]
        - cols_of[None, :]
        + WIN
        - 1
    )


def token_of_row(is_second):
    row = jnp.arange(ROWS, dtype=jnp.int32)
    window, place = row // PW, row % PW
    shift = jnp.where(is_second, SHIFT, 0)
    r = (window // 2 * WIN + place // WIN + shift) % SIDE
    c = (window % 2 * WIN + place % WIN + shift) % SIDE
    return jnp.where(place < WT, r * SIDE + c, -1)


def pad_pairs(values):
    lead = [(0, 0)] * (values.ndim - 2)
    return jnp.pad(jnp.swapaxes(values, -1, -2), lead + [(0, PW - WT), (0, PW - WT)])


def shards(
    images, counts, shift_mask, cotangent, attention_gain, attention_shift, heads_weight,
    query_bias, value_bias, merge_weight, merge_bias, feed_gain, feed_shift, up_weight, up_bias,
    down_weight, down_bias, bias_table,
):
    owners = lax.axis_size("dp")
    grid_ok = owners == 16
    part = C // owners
    is_second = lax.axis_index("section") == 1
    micro = images.shape[0]
    live_rows = (jnp.arange(images.shape[1], dtype=jnp.int32)[None, :] < counts).astype(F32)

    tiles = jnp.concatenate(
        [
            heads_weight[0].reshape(part, 3, C).transpose(1, 0, 2),
            merge_weight[0][None],
            up_weight[0].reshape(part, 4, C).transpose(1, 0, 2),
            down_weight[0].reshape(4, part, C),
        ]
    )
    own_up_size = FF // owners
    vector = jnp.concatenate(
        [
            attention_gain[0], attention_shift[0], query_bias[0], value_bias[0], merge_bias[0],
            feed_gain[0], feed_shift[0], down_bias[0], up_bias[0],
        ]
    )
    vector = jnp.pad(vector, (0, part * C - vector.size)).reshape(1, part, C)
    weights = gather(jnp.concatenate([tiles, vector]), grid_ok)
    vectors = weights[:, TILES].reshape(owners, part * C)[:, : 8 * part + own_up_size].astype(F32)
    wide = vectors[:, : 8 * part].reshape(owners, 8, part).transpose(1, 0, 2).reshape(8, C)
    up_row = vectors[:, 8 * part :].reshape(1, FF)
    vec = wide[jnp.array([0, 1, 4, 5, 6, 7, 7, 7])]
    project_row = jnp.concatenate([wide[2], jnp.zeros_like(wide[2]), wide[3]])[None]

    token = token_of_row(is_second)
    perm = (token[:, None] == jnp.arange(TOKIMG, dtype=jnp.int32)[None, :]).astype(BF16)
    permt = perm.T
    one_hot = (
        relative_index().reshape(-1)[:, None] == jnp.arange(TABLE, dtype=jnp.int32)[None, :]
    ).astype(F32)
    position = jnp.dot(one_hot, bias_table[0].astype(F32), precision=lax.Precision.HIGHEST)
    position = position.reshape(WT, WT, HEADS).transpose(2, 0, 1)
    position = pad_pairs(position).reshape(GROUPS, 4, PW, PW).transpose(0, 2, 1, 3)
    mask = pad_pairs(-100.0 * is_second.astype(F32) * shift_mask.astype(F32))
    edge = jnp.where(jnp.arange(PW) < WT, 0.0, -1e30)[:, None, None]
    bias = position[None] + mask[:, None, :, None, :] + edge
    bias = bias.reshape(NWIN * GROUPS, PW, 4 * PW)

    tick_bf16 = jnp.zeros((TOKIMG, C), BF16)
    received = tick_bf16
    kept, outputs = [], []
    layer_flops = 2 * ROWS * C * C * TILES
    for tick in range(micro + 1):
        own = images[tick, 0] if tick < micro else tick_bf16
        first = live_rows[tick, 0] if tick < micro else 0.0
        second = live_rows[tick - 1, 0] if tick > 0 else 0.0
        live = jnp.where(is_second, second, first).reshape(1, 1)
        source = jnp.where(is_second, received, own)
        out, *stored = call(
            forward_body,
            [
                ((TOKIMG, C), BF16), ((ROWS, C), BF16), ((ROWS, C), BF16), ((ROWS, 3 * C), BF16),
                ((NWIN * GROUPS, PW, 4 * PW), BF16), ((ROWS, C), BF16), ((ROWS, C), F32),
                ((ROWS, C), BF16), ((ROWS, FF), BF16), ((ROWS, FF), BF16),
            ],
            (source, live, perm, permt, bias, weights, vec, project_row, up_row),
            smem=(1,),
            flops=layer_flops,
        )
        kept.append((stored, live))
        outputs.append(out)
        if tick < micro:
            received = lax.ppermute(out, "section", [(0, 1)])
    layer_outputs = jnp.stack(
        [jnp.where(is_second, outputs[m + 1], outputs[m]) for m in range(micro)]
    )[None, :, None]

    received = tick_bf16
    products, grads = [], []
    vec_total = up_total = pair_total = 0.0
    for turn in range(micro + 1):
        (xw, h, qkv, a, r, x1, h2, z, gp), live = kept[micro - turn]
        own = cotangent[micro - 1 - turn, 0] if turn < micro else tick_bf16
        upstream = jnp.where(is_second, own, received)
        dx, sent, do, dg, db, dp, vg, ug, ds = call(
            backward_body,
            [
                ((TOKIMG, C), F32), ((TOKIMG, C), BF16), ((ROWS, C), BF16), ((ROWS, FF), BF16),
                ((ROWS, C), BF16), ((ROWS, 3 * C), BF16), ((8, C), F32), ((1, FF), F32),
                ((GROUPS, PW, 4 * PW), F32),
            ],
            (upstream, live, perm, permt, weights, vec, xw, qkv, a, x1, gp),
            scratch=(pltpu.VMEM((ROWS, C), BF16),),
            smem=(1,),
            flops=layer_flops,
        )
        products.append((h, r, h2, z, do, dg, db, dp))
        vec_total, up_total, pair_total = vec_total + vg, up_total + ug, pair_total + ds
        grads.append(jnp.where(is_second, sent.astype(F32), dx))
        if turn < micro:
            received = lax.ppermute(sent, "section", [(1, 0)])
    input_grads = jnp.stack(
        [
            jnp.where(is_second, grads[micro - 1 - m], grads[micro - m]) for m in range(micro)
        ]
    )[None, :, None]

    count = micro + 1
    pairs = pair_total.reshape(GROUPS, PW, 4, PW)[:, :WT, :, :WT]
    pairs = pairs.transpose(3, 1, 0, 2).reshape(WT * WT, HEADS)
    table = jnp.dot(one_hot.T, pairs, precision=lax.Precision.HIGHEST).reshape(1, -1)
    extra = jnp.concatenate(
        [
            vec_total.reshape(8, owners, part).transpose(1, 0, 2).reshape(owners, 8 * part),
            up_total.reshape(owners, own_up_size),
            jnp.broadcast_to(table, (owners, table.size)),
        ],
        1,
    ).astype(BF16)
    more = -(-extra.shape[1] // (part * C))
    extra = jnp.pad(extra, ((0, 0), (0, more * part * C - extra.shape[1])))
    extra = extra.reshape(owners, more, part, C)
    (tile_grads,) = call(
        lambda *refs: weight_grads_body(count, *refs),
        [((owners, TILES + more, part, C), BF16)],
        tuple(p[i] for i in range(8) for p in products) + (extra,),
        flops=layer_flops * count,
    )
    own_tiles = scatter_sum(tile_grads, grid_ok)
    flat = own_tiles[TILES:].reshape(-1)
    own_vec = flat[: 8 * part].reshape(8, part)
    own_up = flat[8 * part : 8 * part + own_up_size]
    start = 8 * part + own_up_size
    table = flat[start : start + TABLE * HEADS].reshape(1, TABLE, HEADS)
    return (
        layer_outputs,
        input_grads,
        own_vec[0][None],
        own_vec[1][None],
        own_tiles[0:3].transpose(1, 0, 2).reshape(1, part, 3 * C),
        own_vec[2][None],
        own_vec[3][None],
        own_tiles[3][None],
        own_vec[4][None],
        own_vec[5][None],
        own_vec[6][None],
        own_tiles[4:8].transpose(1, 0, 2).reshape(1, part, FF),
        own_up[None],
        own_tiles[8:12].reshape(1, 4 * part, C),
        own_vec[7][None],
        table,
    )


def solution(mesh):
    rows, matrix = P("section", "dp"), P("section", "dp", None)
    tokens = P("section", None, "dp", None, None)
    table = P("section", None, None)
    images = P(None, "dp", None, None)
    return jax.shard_map(
        shards,
        mesh=mesh,
        in_specs=(
            images, P(None, "dp"), P(), images, rows, rows, matrix, rows, rows, matrix, rows,
            rows, rows, matrix, rows, matrix, rows, table,
        ),
        out_specs=(
            tokens, tokens, rows, rows, matrix, rows, rows, matrix, rows, rows, rows, matrix,
            rows, matrix, rows, table,
        ),
        check_vma=False,
    )
```
